32 devices in a mesh: grp: 2 (over y), doc: 4 (over z), proj: 2 (over x), sub: 2 (over core).
Axes of the slice: x: 2, y: 2, z: 4, core: 2. Of those that a mesh axis runs over, the one named last changes fastest.
Arguments:
- hidden_acts: bfloat16 [16384, 11008], P(('grp', 'doc'), ('proj', 'sub')), parts along dimension 0, may hold values from -6 to 6
- out_grads: bfloat16 [16384, 4096], P(('grp', 'doc'), ('proj', 'sub')), parts along dimension 0, may hold values from -6 to 6
- proj_in: bfloat16 [11008, 64], P(('proj', 'sub')), may hold values from -0.0546875 to 0.0546875
- proj_out: bfloat16 [4096, 64], P(('proj', 'sub')), may hold values from -0.09375 to 0.09375
- basis_in: float32 [64, 64], replicated, may hold values from -0.75 to 0.75
- basis_out: float32 [64, 64], replicated, may hold values from -0.75 to 0.75
- eigen_values: float32 [64, 64], P(('proj', 'sub')), may hold values from 0.05 to 2
- block_tokens: int32 [32], P(('grp', 'doc')), parts along dimension 0, may hold values from 1 to 4
- pair_list: int32 [32, 2], P(('grp', 'doc')), parts along dimension 0, may hold values from 0 to 15, as said below
Outputs:
- influence: float32 [4096], P(('grp', 'doc')), parts along dimension 0
The draws below stay inside these ranges and needn't reach their ends.
There are 2 independent parts, one for each index of `grp`. The reference program is written for one: setup_inputs(seed, part) draws one part's arguments, and reference() takes and returns one part's arrays. A program takes and returns all parts, laid end to end along the dimension named above; an argument that names none is the same for every part. Nothing has to cross between parts.
Inputs may be any that keep to these rules, and one draw needn't show every extreme that they name: `pair_list`: rows 4 * i to 4 * (i + 1) - 1 belong to index i of doc: their first block is one of blocks 4 * i to 4 * (i + 1) - 1, their second block lies on another index of doc; no ordered pair appears twice; in these rows exactly 2 pairs have their second block on each of 2 indices of doc and none on the others.
All inputs are finite; a program needn't handle non-finite values.
Results may differ from the reference program's by a relative error of at most 0.00055.
Values may be sent and summed in bfloat16 or wider, within the bound.
A program may use at most 64 MiB of HBM per device.

```python
import math
import jax
import jax.numpy as jnp
from jax import lax

D = 4096
FF = 11008
RANK = 64
DOCB = 128
TOK_DOC = 4
BLK_DEV = 4
CAP = 2
PEERS = 2
PAIR_DEV = 4
BLOCKS = 16
TOKENS = 8192
N_DOC = 4


def draw_pair_list(key, part):
    key = jax.random.fold_in(key, 11)

    def device_rows(device):
        own_key = jax.random.fold_in(key, device)
        offsets = 1 + jax.random.permutation(jax.random.fold_in(own_key, 1), N_DOC - 1)[:PEERS]
        owners = (device + offsets) % N_DOC
        cell_keys = jax.random.split(jax.random.fold_in(own_key, 2), PEERS)
        cells = jax.vmap(lambda k: jax.random.permutation(k, BLK_DEV * BLK_DEV)[:CAP])(cell_keys)
        first = device * BLK_DEV + cells // BLK_DEV
        second = owners[:, None] * BLK_DEV + cells % BLK_DEV
        return jnp.stack([first.reshape(-1), second.reshape(-1)], axis=-1)
    rows = jax.vmap(device_rows)(jnp.arange(N_DOC, dtype=jnp.int32))
    return rows.reshape(N_DOC * PAIR_DEV, 2).astype(jnp.int32)


def plant(drawn, key, low, largest):
    place = [jax.random.randint(jax.random.fold_in(key, axis), (), 0, length) for axis, length in enumerate(drawn.shape)]
    longest = drawn.shape.index(max(drawn.shape))
    neighbour = place[:longest] + [(place[longest] + 1) % drawn.shape[longest]] + place[longest + 1:]
    return drawn.at[tuple(place)].set(low).at[tuple(neighbour)].set(largest)


def levels(rng, dims, cuts, smallest, largest):
    def one(dim, blocks):
        draws = jax.random.uniform(jax.random.fold_in(jax.random.fold_in(rng, 6), dim), (blocks,), jnp.float32, smallest / len(cuts), largest / len(cuts))
        return jnp.repeat(jnp.exp(draws), dims[dim] // blocks).reshape((-1,) + (1,) * (len(dims) - dim - 1))

    gain = one(*cuts[0])
    for cut in cuts[1:]:
        gain = gain * one(*cut)
    return gain


def bell_draw(rng, extent, width, reach, pieces=(), held_as=jnp.bfloat16):
    gain = levels(rng, extent, pieces, -0.22, 0.18) if pieces else 1.0
    drawn = jax.random.normal(rng, extent, jnp.float32) * width * gain
    return jnp.minimum(jnp.maximum(drawn, -reach), reach).astype(held_as)


def setup_inputs(seed: int = 0, part: int = 0) -> dict:
    key_list = jax.random.split(jax.random.key(seed), 10)
    own_keys = jax.random.split(jax.random.fold_in(key_list[9], part), 10)
    hidden_acts = bell_draw(own_keys[0], (TOKENS, FF), 1.0, 6.0, ((0, 4), (1, 4)))
    out_grads = bell_draw(own_keys[1], (TOKENS, D), 1.0, 6.0, ((0, 4), (1, 4)))
    proj_in = bell_draw(key_list[2], (FF, RANK), FF ** -0.5, 0.0546875, ((0, 4),))
    proj_out = bell_draw(key_list[3], (D, RANK), D ** -0.5, 0.09375, ((0, 4),))
    basis_in = bell_draw(key_list[4], (RANK, RANK), RANK ** -0.5, 0.75, (), jnp.float32)
    basis_out = bell_draw(key_list[5], (RANK, RANK), RANK ** -0.5, 0.75, (), jnp.float32)
    eigen_values = jnp.clip(jnp.exp(math.log(2.0) - 3.6888794 * jax.random.uniform(key_list[6], (RANK, RANK), jnp.float32) ** levels(key_list[6], (RANK, RANK), ((0, 4),), -0.2, 0.2)), 0.05, 2.0)
    block_tokens = plant(jax.random.randint(own_keys[7], (BLOCKS,), 1, TOK_DOC + 1), jax.random.fold_in(own_keys[7], 1), 1, TOK_DOC).astype(jnp.int32)
    pair_list = draw_pair_list(jax.random.fold_in(jax.random.fold_in(key_list[9], part), 71), part)
    return {"hidden_acts": hidden_acts, "out_grads": out_grads, "proj_in": proj_in, "proj_out": proj_out, "basis_in": basis_in, "basis_out": basis_out, "eigen_values": eigen_values, "block_tokens": block_tokens, "pair_list": pair_list}


DAMPING = 0.01


def reference(hidden_acts, out_grads, proj_in, proj_out, basis_in, basis_out, eigen_values, block_tokens, pair_list):
    input_fac = jnp.dot(hidden_acts, proj_in, preferred_element_type=jnp.float32)
    output_fac = jnp.dot(out_grads, proj_out, preferred_element_type=jnp.float32)
    input_rot = jnp.dot(input_fac, basis_in, precision=lax.Precision.HIGHEST)
    output_rot = jnp.dot(output_fac, basis_out, precision=lax.Precision.HIGHEST)
    blocks = block_tokens.shape[0]
    valid = (jnp.arange(TOK_DOC, dtype=jnp.int32)[None, :] < block_tokens[:, None]).astype(jnp.float32)
    masked = input_rot.reshape(blocks, DOCB, TOK_DOC, RANK) * valid[:, None, :, None]
    out_form = output_rot.reshape(blocks, DOCB, TOK_DOC, RANK)
    summed = jnp.einsum("bdtr,bdtc->bdrc", out_form, masked, precision=lax.Precision.HIGHEST)
    summed = summed / block_tokens.astype(jnp.float32)[:, None, None, None]
    grads = summed.reshape(blocks, DOCB, RANK * RANK).astype(jnp.bfloat16)
    precond = (grads.astype(jnp.float32) / (eigen_values.reshape(-1) + DAMPING)).astype(jnp.bfloat16)

    def one_pair(pair):
        tile = jnp.dot(precond[pair[0]], grads[pair[1]].T, preferred_element_type=jnp.float32)
        squares = tile * tile
        return jnp.sum(squares, axis=1), jnp.sum(squares, axis=0)

    row_energy, col_energy = lax.map(one_pair, pair_list)
    energy = jnp.zeros((blocks, DOCB), jnp.float32)
    energy = energy.at[pair_list[:, 0]].add(row_energy)
    energy = energy.at[pair_list[:, 1]].add(col_energy)
    return jnp.log1p(energy).reshape(-1)
```

```python
import functools

import jax
import jax.numpy as jnp
from jax import lax
from jax.experimental import pallas as pl
from jax.experimental.pallas import tpu as pltpu
from jax.sharding import PartitionSpec as P

DOCB = 128
TOK_DOC = 4
CAP = 2
DAMPING = 0.01
LANES = 128
MESH = pl.DeviceIdType.MESH
F32 = jnp.float32
BF16 = jnp.bfloat16


def contract_last(a, b):
    return lax.dot_general(a, b, (((1,), (1,)), ((), ())), preferred_element_type=F32)


def split_bf16(x):
    high = x.astype(BF16)
    return high, (x - high.astype(F32)).astype(BF16)


def kernel(
    sizes,
    hid_hbm,
    og_hbm,
    pin_hbm,
    pout_hbm,
    bin_ref,
    bout_ref,
    eig_ref,
    tok_ref,
    pair_ref,
    out_ref,
    hid,
    og,
    pin,
    pout,
    win,
    wout,
    part,
    rs,
    scale,
    red,
    ask_out,
    ask_in,
    eig_all,
    zsend,
    nsend,
    near,
    fsend,
    far,
    fac,
    rot,
    grad_a,
    grad_b,
    precond,
    contrib,
    energy,
    load_sem,
    weight_sem,
    small_send,
    ask_recv,
    eig_recv,
    rs_send,
    rs_recv,
    z_send,
    z_recv,
    n_send,
    n_recv,
    f_send,
    f_recv,
    e_send,
    e_recv,
    *zrecv,
):
    docs, groups, subs, chunks, blocks, rank = sizes
    rows = DOCB * TOK_DOC // chunks
    piece = rows // groups
    pairs = pair_ref.shape[0]
    my_doc = lax.axis_index("doc")
    me = lax.axis_index("proj") * subs + lax.axis_index("sub")

    def group_peer(step):
        return lax.rem(me + step, groups)

    def doc_peer(step):
        return lax.rem(my_doc + step, docs)

    def device(doc, member):
        return {"doc": doc, "proj": lax.div(member, subs), "sub": lax.rem(member, subs)}

    def remote(src, dst, send, recv, doc, member):
        return pltpu.make_async_remote_copy(
            src_ref=src,
            dst_ref=dst,
            send_sem=send,
            recv_sem=recv,
            device_id=device(doc, member),
            device_id_type=MESH,
        )

    weight_copies = [
        pltpu.make_async_copy(pin_hbm, pin, weight_sem.at[0]),
        pltpu.make_async_copy(pout_hbm, pout, weight_sem.at[1]),
    ]
    for copy in weight_copies:
        copy.start()
    loads = []
    for q in range(chunks):
        for k in range(blocks):
            source = pl.ds(k * DOCB * TOK_DOC + q * rows, rows)
            loads.append(
                pltpu.make_async_copy(hid_hbm.at[source], hid.at[q, k], load_sem.at[q, k, 0])
            )
            loads.append(
                pltpu.make_async_copy(og_hbm.at[source], og.at[q, k], load_sem.at[q, k, 1])
            )
    for copy in loads:
        copy.start()

    others = docs * groups
    barrier = pltpu.get_barrier_semaphore()

    def each_other(action):
        if others <= 16:
            for index in range(1, others):
                action(doc_peer(index // groups), group_peer(index % groups))
        else:

            def step(index, carry):
                action(doc_peer(lax.div(index, groups)), group_peer(lax.rem(index, groups)))
                return carry

            lax.fori_loop(1, others, step, 0)

    each_other(
        lambda doc, member: pl.semaphore_signal(
            barrier, inc=1, device_id=device(doc, member), device_id_type=MESH
        )
    )

    firsts = [lax.rem(pair_ref[p, 0], blocks) for p in range(pairs)]
    seconds = [pair_ref[p, 1] for p in range(pairs)]
    owners = [lax.div(b, blocks) for b in seconds]
    slots = []
    for p in range(pairs):
        slot = jnp.int32(0)
        for earlier in range(p):
            slot = slot + jnp.where(owners[earlier] == owners[p], 1, 0)
        slots.append(jnp.minimum(slot, CAP - 1))
    for step in range(1, docs):
        doc = doc_peer(step)
        for s in range(CAP):
            want = jnp.int32(0)
            for p in range(pairs):
                hit = (owners[p] == doc) & (slots[p] == s)
                want = want + jnp.where(hit, lax.rem(seconds[p], blocks), 0)
            ask_out[doc, s] = jnp.full((8, LANES), want, jnp.int32)

    token = lax.rem(lax.broadcasted_iota(jnp.int32, (piece, LANES), 0), TOK_DOC)
    input_half = lax.broadcasted_iota(jnp.int32, (piece, LANES), 1) < rank
    for k in range(blocks):
        count = jnp.full((piece, LANES), tok_ref[k], jnp.int32)
        live = jnp.where(token < count, 1.0 / count.astype(F32), 0.0)
        scale[k] = jnp.where(input_half, live, 1.0)

    half = eig_ref.shape[0] // 2
    even = eig_ref[pl.ds(0, half, stride=2), :]
    odd = eig_ref[pl.ds(1, half, stride=2), :]
    eig_all[me] = jnp.concatenate([even, odd], axis=1)

    zero_in = jnp.zeros((rank, rank), F32)
    basis = jnp.concatenate(
        [
            jnp.concatenate([bin_ref[...], zero_in], axis=1),
            jnp.concatenate([zero_in, bout_ref[...]], axis=1),
        ],
        axis=0,
    )
    basis_high, basis_low = split_bf16(basis.T)

    for copy in weight_copies:
        copy.wait()
    win[...] = jnp.concatenate([pin[...], jnp.zeros_like(pin)], axis=1)
    wout[...] = jnp.concatenate([jnp.zeros_like(pout), pout[...]], axis=1)

    def project(q):
        for copy in loads[2 * blocks * q : 2 * blocks * (q + 1)]:
            copy.wait()
        for k in range(blocks):
            summed = jnp.dot(hid[q, k], win[...], preferred_element_type=F32) + jnp.dot(
                og[q, k], wout[...], preferred_element_type=F32
            )
            part[q, :, k] = summed.astype(BF16).reshape(groups, piece, LANES)

    def rs_copy(q, step):
        peer = group_peer(step)
        return remote(
            part.at[q, peer], rs.at[q, me], rs_send.at[q, peer], rs_recv.at[q, me], my_doc, peer
        )

    def arrived(ref, sem):
        pltpu.make_async_copy(ref, ref, sem).wait()

    def send_parts(q):
        for step in range(1, groups):
            rs_copy(q, step).start()

    def ask_copy(step):
        doc = doc_peer(step)
        return remote(
            ask_out.at[doc], ask_in.at[my_doc], small_send.at[0, doc], ask_recv.at[my_doc], doc, me
        )

    def eig_copy(step):
        peer = group_peer(step)
        return remote(
            eig_all.at[me], eig_all.at[me], small_send.at[1, peer], eig_recv.at[me], my_doc, peer
        )

    def z_copy(q, step):
        doc = doc_peer(step)
        return remote(
            zsend.at[q, doc], zrecv[q].at[my_doc], z_send.at[q, doc], z_recv.at[q, my_doc], doc, me
        )

    def near_copy(q, step):
        peer = group_peer(step)
        return remote(
            nsend.at[q, peer], near.at[q, me], n_send.at[q, peer], n_recv.at[q, me], my_doc, peer
        )

    def far_copy(q, step):
        peer = group_peer(step)
        return remote(
            fsend.at[q, peer], far.at[q, me], f_send.at[q, peer], f_recv.at[q, me], my_doc, peer
        )

    def reduce(q):
        total = part[q, me].astype(F32)
        for step in range(1, groups):
            peer = group_peer(step)
            arrived(rs.at[q, peer], rs_recv.at[q, peer])
            total = total + rs[q, peer].astype(F32)
        total = total * scale[...]
        red[q] = total.astype(BF16)
        for step in range(1, docs):
            doc = doc_peer(step)
            if q == 0:
                arrived(ask_in.at[doc], ask_recv.at[doc])
            for s in range(CAP):
                want = ask_in[doc, s][:1]
                chosen = jnp.zeros((piece, LANES), F32)
                for k in range(blocks):
                    chosen = jnp.where(want == k, total[k], chosen)
                zsend[q, doc, s] = chosen.astype(BF16)
            z_copy(q, step).start()
        for p in range(groups):
            nsend[q, p] = red[q, firsts[p]]
        near[q, me] = nsend[q, me]
        for step in range(1, groups):
            near_copy(q, step).start()

    def send_far(q):
        for step in range(1, docs):
            doc = doc_peer(step)
            arrived(zrecv[q].at[doc], z_recv.at[q, doc])
        for p in range(groups):
            fsend[q, p] = zrecv[q][owners[p], slots[p]]
        far[q, me] = fsend[q, me]
        for step in range(1, groups):
            far_copy(q, step).start()

    def outer(block, target):
        fac[...] = block.reshape(DOCB * TOK_DOC, LANES).astype(F32)
        ordered = jnp.concatenate(
            [fac[pl.ds(t, DOCB, stride=TOK_DOC), :].astype(BF16) for t in range(TOK_DOC)], axis=0
        )
        rot[...] = contract_last(basis_high, ordered) + contract_last(basis_low, ordered)
        inputs = [rot[:rank, t * DOCB : (t + 1) * DOCB] for t in range(TOK_DOC)]
        for r in range(rank):
            total = None
            for t in range(TOK_DOC):
                row = rot[rank + r : rank + r + 1, t * DOCB : (t + 1) * DOCB]
                term = row * inputs[t]
                total = term if total is None else total + term
            target[r * rank : (r + 1) * rank, :] = total.astype(BF16)

    project(0)
    pl.semaphore_wait(barrier, others - 1)
    for step in range(1, docs):
        ask_copy(step).start()
    for step in range(1, groups):
        eig_copy(step).start()
    send_parts(0)
    for q in range(1, chunks):
        project(q)
        send_parts(q)
        reduce(q - 1)
        if q >= 2:
            send_far(q - 2)
    reduce(chunks - 1)
    if chunks >= 2:
        send_far(chunks - 2)

    for step in range(1, groups):
        peer = group_peer(step)
        arrived(eig_all.at[peer], eig_recv.at[peer])
        for q in range(chunks):
            arrived(near.at[q, peer], n_recv.at[q, peer])
    outer(near[...], grad_a)
    one_hot = (
        lax.broadcasted_iota(jnp.int32, (DOCB, DOCB), 0)
        == lax.broadcasted_iota(jnp.int32, (DOCB, DOCB), 1)
    ).astype(BF16)
    for j in range(rank * rank // LANES):
        columns = slice(j * LANES, (j + 1) * LANES)
        turned = contract_last(one_hot, grad_a[columns, :])
        weight = eig_all[j // half, j % half : j % half + 1, :] + DAMPING
        precond[:, columns] = (turned / weight).astype(BF16)

    send_far(chunks - 1)
    for step in range(1, groups):
        peer = group_peer(step)
        for q in range(chunks):
            arrived(far.at[q, peer], f_recv.at[q, peer])
    outer(far[...], grad_b)
    tile = jnp.dot(precond[...], grad_b[...], preferred_element_type=F32)
    squares = tile * tile
    column_energy = jnp.sum(squares, axis=0, keepdims=True)
    row_energy = jnp.sum(squares.T, axis=0, keepdims=True)

    first, second = pair_ref[me, 0], pair_ref[me, 1]
    order = lax.broadcasted_iota(jnp.int32, (blocks, LANES), 0)
    for doc in range(docs):
        index = order + doc * blocks
        contrib[doc] = jnp.where(index == first, row_energy, 0.0) + jnp.where(
            index == second, column_energy, 0.0
        )
    energy[my_doc, me] = contrib[my_doc]

    def energy_copy(doc, member):
        return remote(
            contrib.at[doc],
            energy.at[my_doc, me],
            e_send.at[doc, member],
            e_recv.at[my_doc, me],
            doc,
            member,
        )

    each_other(lambda doc, member: energy_copy(doc, member).start())
    for step in range(1, docs):
        ask_copy(step).wait_send()
        for q in range(chunks):
            z_copy(q, step).wait_send()
    for step in range(1, groups):
        eig_copy(step).wait_send()
        for q in range(chunks):
            rs_copy(q, step).wait_send()
            near_copy(q, step).wait_send()
            far_copy(q, step).wait_send()
    each_other(lambda doc, member: arrived(energy.at[doc, member], e_recv.at[doc, member]))
    total = jnp.sum(energy[...].reshape(others, blocks, LANES), axis=0)
    out_ref[...] = jnp.log1p(total)
    each_other(lambda doc, member: energy_copy(doc, member).wait_send())


def body(
    hidden_acts,
    out_grads,
    proj_in,
    proj_out,
    basis_in,
    basis_out,
    eigen_values,
    block_tokens,
    pair_list,
):
    docs = lax.axis_size("doc")
    subs = lax.axis_size("sub")
    groups = lax.axis_size("proj") * subs
    blocks = block_tokens.shape[0]
    rank = basis_in.shape[0]
    block_rows = DOCB * TOK_DOC
    chunks = min(4, block_rows // (16 * groups))
    rows = block_rows // chunks
    piece = rows // groups
    assert pair_list.shape[0] == groups and 2 * rank == LANES
    sizes = (docs, groups, subs, chunks, blocks, rank)
    any_spec = pl.BlockSpec(memory_space=pl.ANY)
    vmem_spec = pl.BlockSpec(memory_space=pltpu.VMEM)
    smem_spec = pl.BlockSpec(memory_space=pltpu.SMEM)
    dma = pltpu.SemaphoreType.DMA
    most = max(docs, groups)
    features = rank * rank
    scratch = [
        pltpu.VMEM((chunks, blocks, rows, hidden_acts.shape[1]), BF16),
        pltpu.VMEM((chunks, blocks, rows, out_grads.shape[1]), BF16),
        pltpu.VMEM(proj_in.shape, BF16),
        pltpu.VMEM(proj_out.shape, BF16),
        pltpu.VMEM((proj_in.shape[0], LANES), BF16),
        pltpu.VMEM((proj_out.shape[0], LANES), BF16),
        pltpu.VMEM((chunks, groups, blocks, piece, LANES), BF16),
        pltpu.VMEM((chunks, groups, blocks, piece, LANES), BF16),
        pltpu.VMEM((blocks, piece, LANES), F32),
        pltpu.VMEM((chunks, blocks, piece, LANES), BF16),
        pltpu.VMEM((docs, CAP, 8, LANES), jnp.int32),
        pltpu.VMEM((docs, CAP, 8, LANES), jnp.int32),
        pltpu.VMEM((groups, eigen_values.shape[0] // 2, LANES), F32),
        pltpu.VMEM((chunks, docs, CAP, piece, LANES), BF16),
        pltpu.VMEM((chunks, groups, piece, LANES), BF16),
        pltpu.VMEM((chunks, groups, piece, LANES), BF16),
        pltpu.VMEM((chunks, groups, piece, LANES), BF16),
        pltpu.VMEM((chunks, groups, piece, LANES), BF16),
        pltpu.VMEM((block_rows, LANES), F32),
        pltpu.VMEM((LANES, block_rows), F32),
        pltpu.VMEM((features, DOCB), BF16),
        pltpu.VMEM((features, DOCB), BF16),
        pltpu.VMEM((DOCB, features), BF16),
        pltpu.VMEM((docs, blocks, LANES), F32),
        pltpu.VMEM((docs, groups, blocks, LANES), F32),
        dma((chunks, blocks, 2)),
        dma((2,)),
        dma((2, most)),
        dma((docs,)),
        dma((groups,)),
        dma((chunks, groups)),
        dma((chunks, groups)),
        dma((chunks, docs)),
        dma((chunks, docs)),
        dma((chunks, groups)),
        dma((chunks, groups)),
        dma((chunks, groups)),
        dma((chunks, groups)),
        dma((docs, groups)),
        dma((docs, groups)),
    ] + [pltpu.VMEM((docs, CAP, piece, LANES), BF16) for _ in range(chunks)]
    influence = pl.pallas_call(
        functools.partial(kernel, sizes),
        out_shape=jax.ShapeDtypeStruct((blocks, LANES), F32),
        in_specs=[any_spec] * 4 + [vmem_spec] * 3 + [smem_spec] * 2,
        out_specs=vmem_spec,
        scratch_shapes=scratch,
        compiler_params=pltpu.CompilerParams(
            collective_id=0, has_side_effects=True, vmem_limit_bytes=48 * 1024 * 1024
        ),
    )(
        hidden_acts,
        out_grads,
        proj_in,
        proj_out,
        basis_in,
        basis_out,
        eigen_values,
        block_tokens,
        pair_list,
    )
    return influence.reshape(-1)


def solution(mesh):
    in_specs = (
        P(("grp", "doc"), ("proj", "sub")),
        P(("grp", "doc"), ("proj", "sub")),
        P(("proj", "sub"), None),
        P(("proj", "sub"), None),
        P(),
        P(),
        P(("proj", "sub"), None),
        P(("grp", "doc")),
        P(("grp", "doc"), None),
    )
    out_specs = P(("grp", "doc"))
    return jax.shard_map(body, mesh=mesh, in_specs=in_specs, out_specs=out_specs, check_vma=False)
```

```python
import functools

import jax
import jax.numpy as jnp
from jax import lax
from jax.experimental import pallas as pl
from jax.experimental.pallas import tpu as pltpu
from jax.sharding import PartitionSpec as P

DOCB = 128
TOK_DOC = 4
CAP = 2
DAMPING = 0.01
LANES = 128
MESH = pl.DeviceIdType.MESH
F32 = jnp.float32
BF16 = jnp.bfloat16


def contract_last(a, b):
    return lax.dot_general(a, b, (((1,), (1,)), ((), ())), preferred_element_type=F32)


def split_bf16(x):
    high = x.astype(BF16)
    return high, (x - high.astype(F32)).astype(BF16)


def kernel(
    sizes,
    hid_hbm,
    og_hbm,
    pin_hbm,
    pout_hbm,
    bin_ref,
    bout_ref,
    eig_ref,
    tok_ref,
    pair_ref,
    out_ref,
    hid,
    og,
    pin,
    pout,
    spread,
    part,
    rs,
    scale,
    red,
    ask_out,
    ask_in,
    eig_all,
    zsend,
    nsend,
    near,
    fsend,
    far,
    rot,
    grad_a,
    grad_b,
    precond,
    contrib,
    energy,
    load_sem,
    weight_sem,
    small_send,
    ask_recv,
    eig_recv,
    rs_send,
    rs_recv,
    z_send,
    z_recv,
    n_send,
    n_recv,
    f_send,
    f_recv,
    e_send,
    e_recv,
    *zrecv,
):
    docs, groups, subs, chunks, blocks, rank = sizes
    rows = DOCB * TOK_DOC // chunks
    cuts = rows // LANES
    shares = groups // cuts
    piece = LANES // shares
    pairs = pair_ref.shape[1]
    my_doc = lax.axis_index("doc")
    me = lax.axis_index("proj") * subs + lax.axis_index("sub")

    def group_peer(step):
        return lax.rem(me + step, groups)

    def doc_peer(step):
        return lax.rem(my_doc + step, docs)

    def device(doc, member):
        return {"doc": doc, "proj": lax.div(member, subs), "sub": lax.rem(member, subs)}

    def remote(src, dst, send, recv, doc, member):
        return pltpu.make_async_remote_copy(
            src_ref=src,
            dst_ref=dst,
            send_sem=send,
            recv_sem=recv,
            device_id=device(doc, member),
            device_id_type=MESH,
        )

    weight_copies = [
        pltpu.make_async_copy(pin_hbm, pin, weight_sem.at[0]),
        pltpu.make_async_copy(pout_hbm, pout, weight_sem.at[1]),
    ]
    for copy in weight_copies:
        copy.start()
    loads = []
    for q in range(chunks):
        for k in range(blocks):
            source = pl.ds(k * DOCB * TOK_DOC + q * rows, rows)
            target = pl.ds(k * rows, rows)
            loads.append(
                pltpu.make_async_copy(
                    hid_hbm.at[:, source], hid.at[q, :, target], load_sem.at[q, k, 0]
                )
            )
            loads.append(
                pltpu.make_async_copy(og_hbm.at[source], og.at[q, target], load_sem.at[q, k, 1])
            )
    for copy in loads:
        copy.start()

    others = docs * groups
    barrier = pltpu.get_barrier_semaphore()

    def each_other(action):
        if others <= 16:
            for index in range(1, others):
                action(doc_peer(index // groups), group_peer(index % groups))
        else:

            def step(index, carry):
                action(doc_peer(lax.div(index, groups)), group_peer(lax.rem(index, groups)))
                return carry

            lax.fori_loop(1, others, step, 0)

    each_other(
        lambda doc, member: pl.semaphore_signal(
            barrier, inc=1, device_id=device(doc, member), device_id_type=MESH
        )
    )

    firsts = [lax.rem(pair_ref[0, p], blocks) for p in range(pairs)]
    seconds = [pair_ref[1, p] for p in range(pairs)]
    owners = [lax.div(b, blocks) for b in seconds]
    slots = []
    for p in range(pairs):
        slot = jnp.int32(0)
        for earlier in range(p):
            slot = slot + jnp.where(owners[earlier] == owners[p], 1, 0)
        slots.append(jnp.minimum(slot, CAP - 1))
    for step in range(1, docs):
        doc = doc_peer(step)
        for s in range(CAP):
            want = jnp.int32(0)
            for p in range(pairs):
                hit = (owners[p] == doc) & (slots[p] == s)
                want = want + jnp.where(hit, lax.rem(seconds[p], blocks), 0)
            ask_out[doc, s] = jnp.full((8, LANES), want, jnp.int32)

    token = lax.rem(lax.broadcasted_iota(jnp.int32, (piece, LANES), 1), TOK_DOC)
    feature = lax.broadcasted_iota(jnp.int32, (piece, LANES), 0) + lax.rem(me, shares) * piece
    input_half = feature < rank
    for k in range(blocks):
        count = jnp.full((piece, LANES), tok_ref[k], jnp.int32)
        live = jnp.where(token < count, 1.0 / count.astype(F32), 0.0)
        scale[k] = jnp.where(input_half, live, 1.0)

    half = eig_ref.shape[0] // 2
    even = eig_ref[pl.ds(0, half, stride=2), :]
    odd = eig_ref[pl.ds(1, half, stride=2), :]
    eig_all[me] = jnp.concatenate([even, odd], axis=1)

    zero_in = jnp.zeros((rank, rank), F32)
    basis = jnp.concatenate(
        [
            jnp.concatenate([bin_ref[...], zero_in], axis=1),
            jnp.concatenate([zero_in, bout_ref[...]], axis=1),
        ],
        axis=0,
    )
    basis_high, basis_low = split_bf16(basis.T)

    line = lax.broadcasted_iota(jnp.int32, spread.shape, 0)
    column = lax.broadcasted_iota(jnp.int32, spread.shape, 1)
    picked = lax.rem(column, DOCB) * TOK_DOC + lax.div(column, DOCB)
    spread[...] = jnp.where(line == picked, 1.0, 0.0).astype(BF16)

    for copy in weight_copies:
        copy.wait()

    def project(q):
        for copy in loads[2 * blocks * q : 2 * blocks * (q + 1)]:
            copy.wait()
        halves = (
            jnp.dot(pin[...], hid[q], preferred_element_type=F32).astype(BF16),
            contract_last(pout[...], og[q]).astype(BF16),
        )
        for k in range(blocks):
            for g in range(groups):
                first = (g % shares) * piece
                start = k * rows + (g // shares) * LANES
                factor = halves[first // rank]
                row = first % rank
                part[q, g, k] = factor[row : row + piece, start : start + LANES]

    def rs_copy(q, step):
        peer = group_peer(step)
        return remote(
            part.at[q, peer], rs.at[q, me], rs_send.at[q, peer], rs_recv.at[q, me], my_doc, peer
        )

    def arrived(ref, sem):
        pltpu.make_async_copy(ref, ref, sem).wait()

    def send_parts(q):
        for step in range(1, groups):
            rs_copy(q, step).start()

    def ask_copy(step):
        doc = doc_peer(step)
        return remote(
            ask_out.at[doc], ask_in.at[my_doc], small_send.at[0, doc], ask_recv.at[my_doc], doc, me
        )

    def eig_copy(step):
        peer = group_peer(step)
        return remote(
            eig_all.at[me], eig_all.at[me], small_send.at[1, peer], eig_recv.at[me], my_doc, peer
        )

    def z_copy(q, step):
        doc = doc_peer(step)
        return remote(
            zsend.at[q, doc], zrecv[q].at[my_doc], z_send.at[q, doc], z_recv.at[q, my_doc], doc, me
        )

    def near_copy(q, step):
        peer = group_peer(step)
        return remote(
            nsend.at[q, peer], near.at[q, me], n_send.at[q, peer], n_recv.at[q, me], my_doc, peer
        )

    def far_copy(q, step):
        peer = group_peer(step)
        return remote(
            fsend.at[q, peer], far.at[q, me], f_send.at[q, peer], f_recv.at[q, me], my_doc, peer
        )

    def reduce(q):
        total = part[q, me].astype(F32)
        for step in range(1, groups):
            peer = group_peer(step)
            arrived(rs.at[q, peer], rs_recv.at[q, peer])
            total = total + rs[q, peer].astype(F32)
        total = total * scale[...]
        red[q] = total.astype(BF16)
        for step in range(1, docs):
            doc = doc_peer(step)
            if q == 0:
                arrived(ask_in.at[doc], ask_recv.at[doc])
            for s in range(CAP):
                want = ask_in[doc, s][:1]
                chosen = jnp.zeros((piece, LANES), F32)
                for k in range(blocks):
                    chosen = jnp.where(want == k, total[k], chosen)
                zsend[q, doc, s] = chosen.astype(BF16)
            z_copy(q, step).start()
        for p in range(groups):
            nsend[q, p] = red[q, firsts[p]]
        near[q, me] = nsend[q, me]
        for step in range(1, groups):
            near_copy(q, step).start()

    def send_far(q):
        for step in range(1, docs):
            doc = doc_peer(step)
            arrived(zrecv[q].at[doc], z_recv.at[q, doc])
        for p in range(groups):
            fsend[q, p] = zrecv[q][owners[p], slots[p]]
        far[q, me] = fsend[q, me]
        for step in range(1, groups):
            far_copy(q, step).start()

    def outer(block, target):
        lanes = block.reshape(chunks * cuts, LANES, LANES)
        joined = jnp.concatenate([lanes[c] for c in range(chunks * cuts)], axis=1)
        ordered = jnp.dot(joined, spread[...], preferred_element_type=F32).astype(BF16)
        rot[...] = jnp.dot(basis_high, ordered, preferred_element_type=F32) + jnp.dot(
            basis_low, ordered, preferred_element_type=F32
        )
        inputs = [rot[:rank, t * DOCB : (t + 1) * DOCB] for t in range(TOK_DOC)]
        for r in range(rank):
            total = None
            for t in range(TOK_DOC):
                row = rot[rank + r : rank + r + 1, t * DOCB : (t + 1) * DOCB]
                term = row * inputs[t]
                total = term if total is None else total + term
            target[r * rank : (r + 1) * rank, :] = total.astype(BF16)

    project(0)
    pl.semaphore_wait(barrier, others - 1)
    for step in range(1, docs):
        ask_copy(step).start()
    for step in range(1, groups):
        eig_copy(step).start()
    send_parts(0)
    for q in range(1, chunks):
        project(q)
        send_parts(q)
        reduce(q - 1)
        if q >= 2:
            send_far(q - 2)
    reduce(chunks - 1)
    if chunks >= 2:
        send_far(chunks - 2)

    for step in range(1, groups):
        peer = group_peer(step)
        arrived(eig_all.at[peer], eig_recv.at[peer])
        for q in range(chunks):
            arrived(near.at[q, peer], n_recv.at[q, peer])
    outer(near[...], grad_a)
    one_hot = (
        lax.broadcasted_iota(jnp.int32, (DOCB, DOCB), 0)
        == lax.broadcasted_iota(jnp.int32, (DOCB, DOCB), 1)
    ).astype(BF16)
    for j in range(rank * rank // LANES):
        columns = slice(j * LANES, (j + 1) * LANES)
        turned = contract_last(one_hot, grad_a[columns, :])
        weight = eig_all[j // half, j % half : j % half + 1, :] + DAMPING
        precond[:, columns] = (turned / weight).astype(BF16)

    send_far(chunks - 1)
    for step in range(1, groups):
        peer = group_peer(step)
        for q in range(chunks):
            arrived(far.at[q, peer], f_recv.at[q, peer])
    outer(far[...], grad_b)
    tile = jnp.dot(precond[...], grad_b[...], preferred_element_type=F32)
    squares = tile * tile
    column_energy = jnp.sum(squares, axis=0, keepdims=True)
    row_energy = jnp.sum(squares.T, axis=0, keepdims=True)

    first, second = pair_ref[0, me], pair_ref[1, me]
    order = lax.broadcasted_iota(jnp.int32, (blocks, LANES), 0)
    for doc in range(docs):
        index = order + doc * blocks
        contrib[doc] = jnp.where(index == first, row_energy, 0.0) + jnp.where(
            index == second, column_energy, 0.0
        )
    energy[my_doc, me] = contrib[my_doc]

    def energy_copy(doc, member):
        return remote(
            contrib.at[doc],
            energy.at[my_doc, me],
            e_send.at[doc, member],
            e_recv.at[my_doc, me],
            doc,
            member,
        )

    each_other(lambda doc, member: energy_copy(doc, member).start())
    for step in range(1, docs):
        ask_copy(step).wait_send()
        for q in range(chunks):
            z_copy(q, step).wait_send()
    for step in range(1, groups):
        eig_copy(step).wait_send()
        for q in range(chunks):
            rs_copy(q, step).wait_send()
            near_copy(q, step).wait_send()
            far_copy(q, step).wait_send()
    each_other(lambda doc, member: arrived(energy.at[doc, member], e_recv.at[doc, member]))
    total = jnp.sum(energy[...].reshape(others, blocks, LANES), axis=0)
    out_ref[...] = jnp.log1p(total)
    each_other(lambda doc, member: energy_copy(doc, member).wait_send())


def body(
    hidden_acts,
    out_grads,
    proj_in,
    proj_out,
    basis_in,
    basis_out,
    eigen_values,
    block_tokens,
    pair_list,
):
    docs = lax.axis_size("doc")
    subs = lax.axis_size("sub")
    groups = lax.axis_size("proj") * subs
    blocks = block_tokens.shape[0]
    rank = basis_in.shape[0]
    block_rows = DOCB * TOK_DOC
    cuts = max(1, groups // (LANES // 16))
    chunks = block_rows // (LANES * cuts)
    rows = block_rows // chunks
    piece = LANES * cuts // groups
    assert pair_list.shape[0] == groups and 2 * rank == LANES
    sizes = (docs, groups, subs, chunks, blocks, rank)
    any_spec = pl.BlockSpec(memory_space=pl.ANY)
    vmem_spec = pl.BlockSpec(memory_space=pltpu.VMEM)
    smem_spec = pl.BlockSpec(memory_space=pltpu.SMEM)
    dma = pltpu.SemaphoreType.DMA
    most = max(docs, groups)
    features = rank * rank
    scratch = [
        pltpu.VMEM((chunks, hidden_acts.shape[1], blocks * rows), BF16),
        pltpu.VMEM((chunks, blocks * rows, out_grads.shape[1]), BF16),
        pltpu.VMEM((rank, hidden_acts.shape[1]), BF16),
        pltpu.VMEM((rank, out_grads.shape[1]), BF16),
        pltpu.VMEM((block_rows, block_rows), BF16),
        pltpu.VMEM((chunks, groups, blocks, piece, LANES), BF16),
        pltpu.VMEM((chunks, groups, blocks, piece, LANES), BF16),
        pltpu.VMEM((blocks, piece, LANES), F32),
        pltpu.VMEM((chunks, blocks, piece, LANES), BF16),
        pltpu.VMEM((docs, CAP, 8, LANES), jnp.int32),
        pltpu.VMEM((docs, CAP, 8, LANES), jnp.int32),
        pltpu.VMEM((groups, eigen_values.shape[0] // 2, LANES), F32),
        pltpu.VMEM((chunks, docs, CAP, piece, LANES), BF16),
        pltpu.VMEM((chunks, groups, piece, LANES), BF16),
        pltpu.VMEM((chunks, groups, piece, LANES), BF16),
        pltpu.VMEM((chunks, groups, piece, LANES), BF16),
        pltpu.VMEM((chunks, groups, piece, LANES), BF16),
        pltpu.VMEM((LANES, block_rows), F32),
        pltpu.VMEM((features, DOCB), BF16),
        pltpu.VMEM((features, DOCB), BF16),
        pltpu.VMEM((DOCB, features), BF16),
        pltpu.VMEM((docs, blocks, LANES), F32),
        pltpu.VMEM((docs, groups, blocks, LANES), F32),
        dma((chunks, blocks, 2)),
        dma((2,)),
        dma((2, most)),
        dma((docs,)),
        dma((groups,)),
        dma((chunks, groups)),
        dma((chunks, groups)),
        dma((chunks, docs)),
        dma((chunks, docs)),
        dma((chunks, groups)),
        dma((chunks, groups)),
        dma((chunks, groups)),
        dma((chunks, groups)),
        dma((docs, groups)),
        dma((docs, groups)),
    ] + [pltpu.VMEM((docs, CAP, piece, LANES), BF16) for _ in range(chunks)]
    influence = pl.pallas_call(
        functools.partial(kernel, sizes),
        out_shape=jax.ShapeDtypeStruct((blocks, LANES), F32),
        in_specs=[any_spec] * 4 + [vmem_spec] * 3 + [smem_spec] * 2,
        out_specs=vmem_spec,
        scratch_shapes=scratch,
        compiler_params=pltpu.CompilerParams(
            collective_id=0, has_side_effects=True, vmem_limit_bytes=61 * 1024 * 1024
        ),
    )(
        hidden_acts.T,
        out_grads,
        proj_in.T,
        proj_out.T,
        basis_in,
        basis_out,
        eigen_values,
        block_tokens,
        pair_list.T,
    )
    return influence.reshape(-1)


def solution(mesh):
    in_specs = (
        P(("grp", "doc"), ("proj", "sub")),
        P(("grp", "doc"), ("proj", "sub")),
        P(("proj", "sub"), None),
        P(("proj", "sub"), None),
        P(),
        P(),
        P(("proj", "sub"), None),
        P(("grp", "doc")),
        P(("grp", "doc"), None),
    )
    out_specs = P(("grp", "doc"))
    return jax.shard_map(body, mesh=mesh, in_specs=in_specs, out_specs=out_specs, check_vma=False)
```

```python
import functools

import jax
import jax.numpy as jnp
from jax import lax
from jax.experimental import pallas as pl
from jax.experimental.pallas import tpu as pltpu
from jax.sharding import PartitionSpec as P

DOCB = 128
TOK_DOC = 4
CAP = 2
DAMPING = 0.01
LANES = 128
MESH = pl.DeviceIdType.MESH
F32 = jnp.float32
BF16 = jnp.bfloat16


def contract_last(a, b):
    return lax.dot_general(a, b, (((1,), (1,)), ((), ())), preferred_element_type=F32)


def split_bf16(x):
    high = x.astype(BF16)
    return high, (x - high.astype(F32)).astype(BF16)


def kernel(
    sizes,
    hid_hbm,
    og_hbm,
    pin_hbm,
    pout_hbm,
    bin_ref,
    bout_ref,
    eig_ref,
    tok_ref,
    pair_ref,
    out_ref,
    hid,
    og,
    pin,
    pout,
    spread,
    part,
    rs,
    scale,
    red,
    ask_out,
    ask_in,
    eig_all,
    zsend,
    nsend,
    near,
    fsend,
    far,
    rot,
    grad_a,
    grad_b,
    precond,
    contrib,
    energy,
    load_sem,
    weight_sem,
    small_send,
    ask_recv,
    eig_recv,
    rs_send,
    rs_recv,
    z_send,
    z_recv,
    n_send,
    n_recv,
    f_send,
    f_recv,
    e_send,
    e_recv,
    *zrecv,
):
    docs, groups, subs, chunks, blocks, rank = sizes
    rows = DOCB * TOK_DOC // chunks
    cuts = rows // LANES
    shares = groups // cuts
    piece = LANES // shares
    pairs = pair_ref.shape[1]
    my_doc = lax.axis_index("doc")
    me = lax.axis_index("proj") * subs + lax.axis_index("sub")

    def group_peer(step):
        return lax.rem(me + step, groups)

    def doc_peer(step):
        return lax.rem(my_doc + step, docs)

    def device(doc, member):
        return {"doc": doc, "proj": lax.div(member, subs), "sub": lax.rem(member, subs)}

    def remote(src, dst, send, recv, doc, member):
        return pltpu.make_async_remote_copy(
            src_ref=src,
            dst_ref=dst,
            send_sem=send,
            recv_sem=recv,
            device_id=device(doc, member),
            device_id_type=MESH,
        )

    weight_copies = [
        pltpu.make_async_copy(pin_hbm, pin, weight_sem.at[0]),
        pltpu.make_async_copy(pout_hbm, pout, weight_sem.at[1]),
    ]
    for copy in weight_copies:
        copy.start()
    loads = []
    for q in range(chunks):
        for k in range(blocks):
            source = pl.ds(k * DOCB * TOK_DOC + q * rows, rows)
            target = pl.ds(k * rows, rows)
            loads.append(
                pltpu.make_async_copy(
                    hid_hbm.at[:, source], hid.at[q, :, target], load_sem.at[q, k, 0]
                )
            )
            loads.append(
                pltpu.make_async_copy(og_hbm.at[source], og.at[q, target], load_sem.at[q, k, 1])
            )
    for copy in loads:
        copy.start()

    others = docs * groups
    barrier = pltpu.get_barrier_semaphore()

    def each_other(action):
        if others <= 16:
            for index in range(1, others):
                action(doc_peer(index // groups), group_peer(index % groups))
        else:

            def step(index, carry):
                action(doc_peer(lax.div(index, groups)), group_peer(lax.rem(index, groups)))
                return carry

            lax.fori_loop(1, others, step, 0)

    each_other(
        lambda doc, member: pl.semaphore_signal(
            barrier, inc=1, device_id=device(doc, member), device_id_type=MESH
        )
    )

    firsts = [lax.rem(pair_ref[0, p], blocks) for p in range(pairs)]
    seconds = [pair_ref[1, p] for p in range(pairs)]
    owners = [lax.div(b, blocks) for b in seconds]
    slots = []
    for p in range(pairs):
        slot = jnp.int32(0)
        for earlier in range(p):
            slot = slot + jnp.where(owners[earlier] == owners[p], 1, 0)
        slots.append(jnp.minimum(slot, CAP - 1))
    for step in range(1, docs):
        doc = doc_peer(step)
        for s in range(CAP):
            want = jnp.int32(0)
            for p in range(pairs):
                hit = (owners[p] == doc) & (slots[p] == s)
                want = want + jnp.where(hit, lax.rem(seconds[p], blocks), 0)
            ask_out[doc, s] = jnp.full((8, LANES), want, jnp.int32)

    token = lax.rem(lax.broadcasted_iota(jnp.int32, (piece, LANES), 1), TOK_DOC)
    feature = lax.broadcasted_iota(jnp.int32, (piece, LANES), 0) + lax.rem(me, shares) * piece
    input_half = feature < rank
    for k in range(blocks):
        count = jnp.full((piece, LANES), tok_ref[k], jnp.int32)
        live = jnp.where(token < count, 1.0 / count.astype(F32), 0.0)
        scale[k] = jnp.where(input_half, live, 1.0)

    half = eig_ref.shape[0] // 2
    even = eig_ref[pl.ds(0, half, stride=2), :]
    odd = eig_ref[pl.ds(1, half, stride=2), :]
    eig_all[me] = jnp.concatenate([even, odd], axis=1)

    zero_in = jnp.zeros((rank, rank), F32)
    basis = jnp.concatenate(
        [
            jnp.concatenate([bin_ref[...], zero_in], axis=1),
            jnp.concatenate([zero_in, bout_ref[...]], axis=1),
        ],
        axis=0,
    )
    basis_high, basis_low = split_bf16(basis.T)

    line = lax.broadcasted_iota(jnp.int32, spread.shape, 0)
    column = lax.broadcasted_iota(jnp.int32, spread.shape, 1)
    picked = lax.rem(column, DOCB) * TOK_DOC + lax.div(column, DOCB)
    spread[...] = jnp.where(line == picked, 1.0, 0.0).astype(BF16)

    for copy in weight_copies:
        copy.wait()

    def project(q):
        for copy in loads[2 * blocks * q : 2 * blocks * (q + 1)]:
            copy.wait()
        halves = (
            jnp.dot(pin[...], hid[q], preferred_element_type=F32).astype(BF16),
            contract_last(pout[...], og[q]).astype(BF16),
        )
        for k in range(blocks):
            for g in range(groups):
                first = (g % shares) * piece
                start = k * rows + (g // shares) * LANES
                factor = halves[first // rank]
                row = first % rank
                part[q, g, k] = factor[row : row + piece, start : start + LANES]

    def rs_copy(q, step):
        peer = group_peer(step)
        return remote(
            part.at[q, peer], rs.at[q, me], rs_send.at[q, peer], rs_recv.at[q, me], my_doc, peer
        )

    def arrived(ref, sem):
        pltpu.make_async_copy(ref, ref, sem).wait()

    def send_parts(q):
        for step in range(1, groups):
            rs_copy(q, step).start()

    def ask_copy(step):
        doc = doc_peer(step)
        return remote(
            ask_out.at[doc], ask_in.at[my_doc], small_send.at[0, doc], ask_recv.at[my_doc], doc, me
        )

    def eig_copy(step):
        peer = group_peer(step)
        return remote(
            eig_all.at[me], eig_all.at[me], small_send.at[1, peer], eig_recv.at[me], my_doc, peer
        )

    def z_copy(q, step):
        doc = doc_peer(step)
        return remote(
            zsend.at[q, doc], zrecv[q].at[my_doc], z_send.at[q, doc], z_recv.at[q, my_doc], doc, me
        )

    def near_copy(step):
        peer = group_peer(step)
        return remote(nsend.at[peer], near.at[me], n_send.at[peer], n_recv.at[me], my_doc, peer)

    def far_copy(q, step):
        peer = group_peer(step)
        return remote(
            fsend.at[peer, q], far.at[me, q], f_send.at[peer, q], f_recv.at[me, q], my_doc, peer
        )

    def reduce(q):
        total = part[q, me].astype(F32)
        for step in range(1, groups):
            peer = group_peer(step)
            arrived(rs.at[q, peer], rs_recv.at[q, peer])
            total = total + rs[q, peer].astype(F32)
        total = total * scale[...]
        red[q] = total.astype(BF16)
        for step in range(1, docs):
            doc = doc_peer(step)
            if q == 0:
                arrived(ask_in.at[doc], ask_recv.at[doc])
            for s in range(CAP):
                want = ask_in[doc, s][:1]
                chosen = jnp.zeros((piece, LANES), F32)
                for k in range(blocks):
                    chosen = jnp.where(want == k, total[k], chosen)
                zsend[q, doc, s] = chosen.astype(BF16)
            z_copy(q, step).start()
        for p in range(groups):
            nsend[p, q] = red[q, firsts[p]]

    def send_far(q):
        for step in range(1, docs):
            doc = doc_peer(step)
            arrived(zrecv[q].at[doc], z_recv.at[q, doc])
        for p in range(groups):
            fsend[p, q] = zrecv[q][owners[p], slots[p]]
        far[me, q] = fsend[me, q]
        for step in range(1, groups):
            far_copy(q, step).start()

    def outer(block, target):
        joined = jnp.concatenate(
            [
                block[cut * shares : (cut + 1) * shares, q].reshape(LANES, LANES)
                for q in range(chunks)
                for cut in range(cuts)
            ],
            axis=1,
        )
        ordered = jnp.dot(joined, spread[...], preferred_element_type=F32).astype(BF16)
        rot[...] = jnp.dot(basis_high, ordered, preferred_element_type=F32) + jnp.dot(
            basis_low, ordered, preferred_element_type=F32
        )
        inputs = [rot[:rank, t * DOCB : (t + 1) * DOCB] for t in range(TOK_DOC)]
        for r in range(rank):
            total = None
            for t in range(TOK_DOC):
                row = rot[rank + r : rank + r + 1, t * DOCB : (t + 1) * DOCB]
                term = row * inputs[t]
                total = term if total is None else total + term
            target[r * rank : (r + 1) * rank, :] = total.astype(BF16)

    project(0)
    pl.semaphore_wait(barrier, others - 1)
    for step in range(1, docs):
        ask_copy(step).start()
    for step in range(1, groups):
        eig_copy(step).start()
    send_parts(0)
    for q in range(1, chunks):
        project(q)
        send_parts(q)
        reduce(q - 1)
        if q >= 2:
            send_far(q - 2)
    reduce(chunks - 1)
    near[me] = nsend[me]
    for step in range(1, groups):
        near_copy(step).start()
    if chunks >= 2:
        send_far(chunks - 2)

    for step in range(1, groups):
        peer = group_peer(step)
        arrived(eig_all.at[peer], eig_recv.at[peer])
        arrived(near.at[peer], n_recv.at[peer])
    outer(near[...], grad_a)
    one_hot = (
        lax.broadcasted_iota(jnp.int32, (DOCB, DOCB), 0)
        == lax.broadcasted_iota(jnp.int32, (DOCB, DOCB), 1)
    ).astype(BF16)
    for j in range(rank * rank // LANES):
        columns = slice(j * LANES, (j + 1) * LANES)
        turned = contract_last(one_hot, grad_a[columns, :])
        weight = eig_all[j // half, j % half : j % half + 1, :] + DAMPING
        precond[:, columns] = (turned / weight).astype(BF16)

    send_far(chunks - 1)
    for step in range(1, groups):
        peer = group_peer(step)
        for q in range(chunks):
            arrived(far.at[peer, q], f_recv.at[peer, q])
    outer(far[...], grad_b)
    tile = jnp.dot(precond[...], grad_b[...], preferred_element_type=F32)
    squares = tile * tile
    column_energy = jnp.sum(squares, axis=0, keepdims=True)
    row_energy = jnp.sum(squares.T, axis=0, keepdims=True)

    first, second = pair_ref[0, me], pair_ref[1, me]
    order = lax.broadcasted_iota(jnp.int32, (blocks, LANES), 0)
    for doc in range(docs):
        index = order + doc * blocks
        contrib[doc] = jnp.where(index == first, row_energy, 0.0) + jnp.where(
            index == second, column_energy, 0.0
        )
    energy[my_doc, me] = contrib[my_doc]

    def energy_copy(doc, member):
        return remote(
            contrib.at[doc],
            energy.at[my_doc, me],
            e_send.at[doc, member],
            e_recv.at[my_doc, me],
            doc,
            member,
        )

    each_other(lambda doc, member: energy_copy(doc, member).start())
    for step in range(1, docs):
        ask_copy(step).wait_send()
        for q in range(chunks):
            z_copy(q, step).wait_send()
    for step in range(1, groups):
        eig_copy(step).wait_send()
        near_copy(step).wait_send()
        for q in range(chunks):
            rs_copy(q, step).wait_send()
            far_copy(q, step).wait_send()
    each_other(lambda doc, member: arrived(energy.at[doc, member], e_recv.at[doc, member]))
    total = jnp.sum(energy[...].reshape(others, blocks, LANES), axis=0)
    out_ref[...] = jnp.log1p(total)
    each_other(lambda doc, member: energy_copy(doc, member).wait_send())


def body(
    hidden_acts,
    out_grads,
    proj_in,
    proj_out,
    basis_in,
    basis_out,
    eigen_values,
    block_tokens,
    pair_list,
):
    docs = lax.axis_size("doc")
    subs = lax.axis_size("sub")
    groups = lax.axis_size("proj") * subs
    blocks = block_tokens.shape[0]
    rank = basis_in.shape[0]
    block_rows = DOCB * TOK_DOC
    cuts = max(2, groups // (LANES // 16))
    chunks = block_rows // (LANES * cuts)
    rows = block_rows // chunks
    piece = LANES * cuts // groups
    assert pair_list.shape[0] == groups and 2 * rank == LANES
    sizes = (docs, groups, subs, chunks, blocks, rank)
    any_spec = pl.BlockSpec(memory_space=pl.ANY)
    vmem_spec = pl.BlockSpec(memory_space=pltpu.VMEM)
    smem_spec = pl.BlockSpec(memory_space=pltpu.SMEM)
    dma = pltpu.SemaphoreType.DMA
    most = max(docs, groups)
    features = rank * rank
    scratch = [
        pltpu.VMEM((chunks, hidden_acts.shape[1], blocks * rows), BF16),
        pltpu.VMEM((chunks, blocks * rows, out_grads.shape[1]), BF16),
        pltpu.VMEM((rank, hidden_acts.shape[1]), BF16),
        pltpu.VMEM((rank, out_grads.shape[1]), BF16),
        pltpu.VMEM((block_rows, block_rows), BF16),
        pltpu.VMEM((chunks, groups, blocks, piece, LANES), BF16),
        pltpu.VMEM((chunks, groups, blocks, piece, LANES), BF16),
        pltpu.VMEM((blocks, piece, LANES), F32),
        pltpu.VMEM((chunks, blocks, piece, LANES), BF16),
        pltpu.VMEM((docs, CAP, 8, LANES), jnp.int32),
        pltpu.VMEM((docs, CAP, 8, LANES), jnp.int32),
        pltpu.VMEM((groups, eigen_values.shape[0] // 2, LANES), F32),
        pltpu.VMEM((chunks, docs, CAP, piece, LANES), BF16),
        pltpu.VMEM((groups, chunks, piece, LANES), BF16),
        pltpu.VMEM((groups, chunks, piece, LANES), BF16),
        pltpu.VMEM((groups, chunks, piece, LANES), BF16),
        pltpu.VMEM((groups, chunks, piece, LANES), BF16),
        pltpu.VMEM((LANES, block_rows), F32),
        pltpu.VMEM((features, DOCB), BF16),
        pltpu.VMEM((features, DOCB), BF16),
        pltpu.VMEM((DOCB, features), BF16),
        pltpu.VMEM((docs, blocks, LANES), F32),
        pltpu.VMEM((docs, groups, blocks, LANES), F32),
        dma((chunks, blocks, 2)),
        dma((2,)),
        dma((2, most)),
        dma((docs,)),
        dma((groups,)),
        dma((chunks, groups)),
        dma((chunks, groups)),
        dma((chunks, docs)),
        dma((chunks, docs)),
        dma((groups,)),
        dma((groups,)),
        dma((groups, chunks)),
        dma((groups, chunks)),
        dma((docs, groups)),
        dma((docs, groups)),
    ] + [pltpu.VMEM((docs, CAP, piece, LANES), BF16) for _ in range(chunks)]
    influence = pl.pallas_call(
        functools.partial(kernel, sizes),
        out_shape=jax.ShapeDtypeStruct((blocks, LANES), F32),
        in_specs=[any_spec] * 4 + [vmem_spec] * 3 + [smem_spec] * 2,
        out_specs=vmem_spec,
        scratch_shapes=scratch,
        compiler_params=pltpu.CompilerParams(
            collective_id=0, has_side_effects=True, vmem_limit_bytes=61 * 1024 * 1024
        ),
    )(
        hidden_acts.T,
        out_grads,
        proj_in.T,
        proj_out.T,
        basis_in,
        basis_out,
        eigen_values,
        block_tokens,
        pair_list.T,
    )
    return influence.reshape(-1)


def solution(mesh):
    in_specs = (
        P(("grp", "doc"), ("proj", "sub")),
        P(("grp", "doc"), ("proj", "sub")),
        P(("proj", "sub"), None),
        P(("proj", "sub"), None),
        P(),
        P(),
        P(("proj", "sub"), None),
        P(("grp", "doc")),
        P(("grp", "doc"), None),
    )
    out_specs = P(("grp", "doc"))
    return jax.shard_map(body, mesh=mesh, in_specs=in_specs, out_specs=out_specs, check_vma=False)
```

```python
import functools

import jax
import jax.numpy as jnp
from jax import lax
from jax.experimental import pallas as pl
from jax.experimental.pallas import tpu as pltpu
from jax.sharding import PartitionSpec as P

DOCB = 128
TOK_DOC = 4
CAP = 2
DAMPING = 0.01
LANES = 128
MESH = pl.DeviceIdType.MESH
F32 = jnp.float32
BF16 = jnp.bfloat16


def contract_last(a, b):
    return lax.dot_general(a, b, (((1,), (1,)), ((), ())), preferred_element_type=F32)


def split_bf16(x):
    high = x.astype(BF16)
    return high, (x - high.astype(F32)).astype(BF16)


def kernel(
    sizes,
    hid_hbm,
    og_hbm,
    pin_hbm,
    pout_hbm,
    bin_ref,
    bout_ref,
    eig_ref,
    tok_ref,
    pair_ref,
    out_ref,
    hid,
    og,
    pin,
    pout,
    spread,
    part,
    rs,
    scale,
    red,
    ask_out,
    ask_in,
    eig_all,
    zsend,
    nsend,
    near,
    fsend,
    far,
    rot,
    grad_a,
    grad_b,
    precond,
    contrib,
    energy,
    load_sem,
    weight_sem,
    small_send,
    ask_recv,
    eig_recv,
    rs_send,
    rs_recv,
    z_send,
    z_recv,
    n_send,
    n_recv,
    f_send,
    f_recv,
    e_send,
    e_recv,
    *zrecv,
):
    docs, groups, subs, chunks, blocks, rank = sizes
    rows = DOCB * TOK_DOC // chunks
    cuts = rows // LANES
    shares = groups // cuts
    piece = LANES // shares
    pairs = pair_ref.shape[1]
    my_doc = lax.axis_index("doc")
    my_proj = lax.axis_index("proj")
    my_sub = lax.axis_index("sub")
    me = my_proj * subs + my_sub

    def wrapped(index, step, size):
        moved = index + step
        return jnp.where(moved >= size, moved - size, moved)

    doc_peers = [wrapped(my_doc, step, docs) for step in range(1, docs)]
    group_peers = []
    places = []
    for step in range(1, groups):
        proj = wrapped(my_proj, step // subs, groups // subs)
        sub = wrapped(my_sub, step % subs, subs)
        group_peers.append(proj * subs + sub)
        places.append({"proj": proj, "sub": sub})

    def doc_peer(step):
        return doc_peers[step - 1]

    def group_peer(step):
        return group_peers[step - 1]

    def owner_of(block):
        return lax.shift_right_logical(block, jnp.int32(blocks.bit_length() - 1))

    def place_of(block):
        return jnp.bitwise_and(block, jnp.int32(blocks - 1))

    def remote(src, dst, send, recv, target):
        return pltpu.make_async_remote_copy(
            src_ref=src,
            dst_ref=dst,
            send_sem=send,
            recv_sem=recv,
            device_id=target,
            device_id_type=MESH,
        )

    weight_copies = [
        pltpu.make_async_copy(pin_hbm, pin, weight_sem.at[0]),
        pltpu.make_async_copy(pout_hbm, pout, weight_sem.at[1]),
    ]
    for copy in weight_copies:
        copy.start()
    loads = []
    for q in range(chunks):
        for k in range(blocks):
            source = pl.ds(k * DOCB * TOK_DOC + q * rows, rows)
            target = pl.ds(k * rows, rows)
            loads.append(
                pltpu.make_async_copy(
                    hid_hbm.at[:, source], hid.at[q, :, target], load_sem.at[q, k, 0]
                )
            )
            loads.append(
                pltpu.make_async_copy(og_hbm.at[source], og.at[q, target], load_sem.at[q, k, 1])
            )
    for copy in loads:
        copy.start()

    barrier = pltpu.get_barrier_semaphore()
    others = docs * groups

    def each_other(action):
        if others <= 16:
            for index in range(1, others):
                far_off, step = index // groups, index % groups
                doc = doc_peers[far_off - 1] if far_off else my_doc
                place = places[step - 1] if step else {"proj": my_proj, "sub": my_sub}
                action(index, doc, {"doc": doc, **place})
        else:

            def move(index, carry):
                doc = wrapped(my_doc, lax.div(index, groups), docs)
                member = wrapped(me, lax.rem(index, groups), groups)
                place = {"proj": lax.div(member, subs), "sub": lax.rem(member, subs)}
                action(index, doc, {"doc": doc, **place})
                return carry

            lax.fori_loop(1, others, move, 0)

    each_other(
        lambda index, doc, target: pl.semaphore_signal(
            barrier, inc=1, device_id=target, device_id_type=MESH
        )
    )

    firsts = [place_of(pair_ref[0, p]) for p in range(pairs)]
    seconds = [pair_ref[1, p] for p in range(pairs)]
    owners = [owner_of(b) for b in seconds]
    slots = []
    for p in range(pairs):
        slot = jnp.int32(0)
        for earlier in range(p):
            slot = slot + jnp.where(owners[earlier] == owners[p], 1, 0)
        slots.append(jnp.minimum(slot, CAP - 1))
    sources = [
        jnp.where(owner >= my_doc, my_doc - owner + docs, my_doc - owner) - 1 for owner in owners
    ]
    sources = [jnp.clip(source, 0, docs - 2) for source in sources]
    for step in range(1, docs):
        doc = doc_peer(step)
        for s in range(CAP):
            want = jnp.int32(0)
            for p in range(pairs):
                hit = (owners[p] == doc) & (slots[p] == s)
                want = want + jnp.where(hit, place_of(seconds[p]), 0)
            ask_out[doc, s] = jnp.full((8, LANES), want, jnp.int32)

    token = jnp.bitwise_and(lax.broadcasted_iota(jnp.int32, (piece, LANES), 1), TOK_DOC - 1)
    feature = lax.broadcasted_iota(jnp.int32, (piece, LANES), 0) + lax.rem(me, shares) * piece
    input_half = feature < rank
    for k in range(blocks):
        count = jnp.full((piece, LANES), tok_ref[k], jnp.int32)
        live = jnp.where(token < count, 1.0 / count.astype(F32), 0.0)
        scale[k] = jnp.where(input_half, live, 1.0)

    half = eig_ref.shape[0] // 2
    even = eig_ref[pl.ds(0, half, stride=2), :]
    odd = eig_ref[pl.ds(1, half, stride=2), :]
    eig_all[me] = jnp.concatenate([even, odd], axis=1)

    zero_in = jnp.zeros((rank, rank), F32)
    basis = jnp.concatenate(
        [
            jnp.concatenate([bin_ref[...], zero_in], axis=1),
            jnp.concatenate([zero_in, bout_ref[...]], axis=1),
        ],
        axis=0,
    )
    basis_high, basis_low = split_bf16(basis.T)

    line = lax.broadcasted_iota(jnp.int32, spread.shape, 0)
    column = lax.broadcasted_iota(jnp.int32, spread.shape, 1)
    picked = jnp.bitwise_and(column, DOCB - 1) * TOK_DOC + lax.shift_right_logical(
        column, DOCB.bit_length() - 1
    )
    spread[...] = jnp.where(line == picked, 1.0, 0.0).astype(BF16)

    for copy in weight_copies:
        copy.wait()

    def project(q):
        for copy in loads[2 * blocks * q : 2 * blocks * (q + 1)]:
            copy.wait()
        halves = (
            jnp.dot(pin[...], hid[q], preferred_element_type=F32).astype(BF16),
            contract_last(pout[...], og[q]).astype(BF16),
        )
        for k in range(blocks):
            for g in range(groups):
                first = (g % shares) * piece
                start = k * rows + (g // shares) * LANES
                factor = halves[first // rank]
                row = first % rank
                part[q, g, k] = factor[row : row + piece, start : start + LANES]

    def rs_copy(q, step):
        peer = group_peer(step)
        return remote(
            part.at[q, peer], rs.at[q, step - 1], rs_send.at[q], rs_recv.at[q], places[step - 1]
        )

    def arrived(ref, sem):
        pltpu.make_async_copy(ref, ref, sem).wait()

    def send_parts(q):
        for step in range(1, groups):
            rs_copy(q, step).start()

    def ask_copy(step):
        doc = doc_peer(step)
        return remote(
            ask_out.at[doc], ask_in.at[step - 1], small_send.at[0], ask_recv, {"doc": doc}
        )

    def eig_copy(step):
        peer = group_peer(step)
        return remote(
            eig_all.at[me], eig_all.at[me], small_send.at[1], eig_recv, places[step - 1]
        )

    def z_copy(q, step):
        doc = doc_peer(step)
        return remote(
            zsend.at[q, doc], zrecv[q].at[step - 1], z_send.at[q], z_recv.at[q], {"doc": doc}
        )

    def near_copy(step):
        peer = group_peer(step)
        return remote(nsend.at[peer], near.at[me], n_send, n_recv, places[step - 1])

    def far_copy(q, step):
        peer = group_peer(step)
        return remote(
            fsend.at[peer, q], far.at[me, q], f_send.at[q], f_recv.at[q], places[step - 1]
        )

    def reduce(q):
        total = part[q, me].astype(F32)
        arrived(rs.at[q], rs_recv.at[q])
        for step in range(1, groups):
            total = total + rs[q, step - 1].astype(F32)
        total = total * scale[...]
        red[q] = total.astype(BF16)
        if q == 0:
            arrived(ask_in, ask_recv)
        for step in range(1, docs):
            doc = doc_peer(step)
            for s in range(CAP):
                want = ask_in[docs - step - 1, s][:1]
                chosen = jnp.zeros((piece, LANES), F32)
                for k in range(blocks):
                    chosen = jnp.where(want == k, total[k], chosen)
                zsend[q, doc, s] = chosen.astype(BF16)
            z_copy(q, step).start()
        for p in range(groups):
            nsend[p, q] = red[q, firsts[p]]

    def send_far(q):
        arrived(zrecv[q], z_recv.at[q])
        for p in range(groups):
            fsend[p, q] = zrecv[q][sources[p], slots[p]]
        far[me, q] = fsend[me, q]
        for step in range(1, groups):
            far_copy(q, step).start()

    def outer(block, target):
        joined = jnp.concatenate(
            [
                block[cut * shares : (cut + 1) * shares, q].reshape(LANES, LANES)
                for q in range(chunks)
                for cut in range(cuts)
            ],
            axis=1,
        )
        ordered = jnp.dot(joined, spread[...], preferred_element_type=F32).astype(BF16)
        rot[...] = jnp.dot(basis_high, ordered, preferred_element_type=F32) + jnp.dot(
            basis_low, ordered, preferred_element_type=F32
        )
        inputs = [rot[:rank, t * DOCB : (t + 1) * DOCB] for t in range(TOK_DOC)]
        for r in range(rank):
            total = None
            for t in range(TOK_DOC):
                row = rot[rank + r : rank + r + 1, t * DOCB : (t + 1) * DOCB]
                term = row * inputs[t]
                total = term if total is None else total + term
            target[r * rank : (r + 1) * rank, :] = total.astype(BF16)

    project(0)
    pl.semaphore_wait(barrier, others - 1)
    send_parts(0)
    for step in range(1, docs):
        ask_copy(step).start()
    for step in range(1, groups):
        eig_copy(step).start()
    for q in range(1, chunks):
        project(q)
        send_parts(q)
        reduce(q - 1)
        if q >= 2:
            send_far(q - 2)
    reduce(chunks - 1)
    near[me] = nsend[me]
    for step in range(1, groups):
        near_copy(step).start()
    if chunks >= 2:
        send_far(chunks - 2)

    group_rest = pl.ds(0, groups - 1)
    doc_rest = pl.ds(0, docs - 1)
    arrived(eig_all.at[group_rest], eig_recv)
    arrived(near.at[group_rest], n_recv)
    outer(near[...], grad_a)
    one_hot = (
        lax.broadcasted_iota(jnp.int32, (DOCB, DOCB), 0)
        == lax.broadcasted_iota(jnp.int32, (DOCB, DOCB), 1)
    ).astype(BF16)
    for j in range(rank * rank // LANES):
        columns = slice(j * LANES, (j + 1) * LANES)
        turned = contract_last(one_hot, grad_a[columns, :])
        weight = eig_all[j // half, j % half : j % half + 1, :] + DAMPING
        precond[:, columns] = (turned / weight).astype(BF16)

    send_far(chunks - 1)
    for q in range(chunks):
        arrived(far.at[group_rest, q], f_recv.at[q])
    outer(far[...], grad_b)
    tile = jnp.dot(precond[...], grad_b[...], preferred_element_type=F32)
    squares = tile * tile
    column_energy = jnp.sum(squares, axis=0, keepdims=True)
    row_energy = jnp.sum(squares.T, axis=0, keepdims=True)

    first, second = pair_ref[0, me], pair_ref[1, me]
    order = lax.broadcasted_iota(jnp.int32, (blocks, LANES), 0)
    for doc in range(docs):
        index = order + doc * blocks
        contrib[doc] = jnp.where(index == first, row_energy, 0.0) + jnp.where(
            index == second, column_energy, 0.0
        )
    def energy_copy(index, doc, target):
        return remote(contrib.at[doc], energy.at[index - 1], e_send, e_recv, target)

    each_other(lambda *peer: energy_copy(*peer).start())
    arrived(ask_out.at[doc_rest], small_send.at[0])
    arrived(eig_all.at[group_rest], small_send.at[1])
    arrived(nsend.at[group_rest], n_send)
    for q in range(chunks):
        arrived(part.at[q, group_rest], rs_send.at[q])
        arrived(zsend.at[q, doc_rest], z_send.at[q])
        arrived(fsend.at[group_rest, q], f_send.at[q])
    arrived(energy, e_recv)
    out_ref[...] = jnp.log1p(contrib[my_doc] + jnp.sum(energy[...], axis=0))
    arrived(energy, e_send)


def body(
    hidden_acts,
    out_grads,
    proj_in,
    proj_out,
    basis_in,
    basis_out,
    eigen_values,
    block_tokens,
    pair_list,
):
    docs = lax.axis_size("doc")
    subs = lax.axis_size("sub")
    groups = lax.axis_size("proj") * subs
    blocks = block_tokens.shape[0]
    rank = basis_in.shape[0]
    block_rows = DOCB * TOK_DOC
    cuts = max(2, groups // (LANES // 16))
    chunks = block_rows // (LANES * cuts)
    rows = block_rows // chunks
    piece = LANES * cuts // groups
    assert blocks & (blocks - 1) == 0
    assert pair_list.shape[0] == groups and 2 * rank == LANES
    sizes = (docs, groups, subs, chunks, blocks, rank)
    any_spec = pl.BlockSpec(memory_space=pl.ANY)
    vmem_spec = pl.BlockSpec(memory_space=pltpu.VMEM)
    smem_spec = pl.BlockSpec(memory_space=pltpu.SMEM)
    dma = pltpu.SemaphoreType.DMA
    features = rank * rank
    scratch = [
        pltpu.VMEM((chunks, hidden_acts.shape[1], blocks * rows), BF16),
        pltpu.VMEM((chunks, blocks * rows, out_grads.shape[1]), BF16),
        pltpu.VMEM((rank, hidden_acts.shape[1]), BF16),
        pltpu.VMEM((rank, out_grads.shape[1]), BF16),
        pltpu.VMEM((block_rows, block_rows), BF16),
        pltpu.VMEM((chunks, groups, blocks, piece, LANES), BF16),
        pltpu.VMEM((chunks, groups - 1, blocks, piece, LANES), BF16),
        pltpu.VMEM((blocks, piece, LANES), F32),
        pltpu.VMEM((chunks, blocks, piece, LANES), BF16),
        pltpu.VMEM((docs, CAP, 8, LANES), jnp.int32),
        pltpu.VMEM((docs - 1, CAP, 8, LANES), jnp.int32),
        pltpu.VMEM((groups, eigen_values.shape[0] // 2, LANES), F32),
        pltpu.VMEM((chunks, docs, CAP, piece, LANES), BF16),
        pltpu.VMEM((groups, chunks, piece, LANES), BF16),
        pltpu.VMEM((groups, chunks, piece, LANES), BF16),
        pltpu.VMEM((groups, chunks, piece, LANES), BF16),
        pltpu.VMEM((groups, chunks, piece, LANES), BF16),
        pltpu.VMEM((LANES, block_rows), F32),
        pltpu.VMEM((features, DOCB), BF16),
        pltpu.VMEM((features, DOCB), BF16),
        pltpu.VMEM((DOCB, features), BF16),
        pltpu.VMEM((docs, blocks, LANES), F32),
        pltpu.VMEM((docs * groups - 1, blocks, LANES), F32),
        dma((chunks, blocks, 2)),
        dma((2,)),
        dma((2,)),
        dma(()),
        dma(()),
        dma((chunks,)),
        dma((chunks,)),
        dma((chunks,)),
        dma((chunks,)),
        dma(()),
        dma(()),
        dma((chunks,)),
        dma((chunks,)),
        dma(()),
        dma(()),
    ] + [pltpu.VMEM((docs - 1, CAP, piece, LANES), BF16) for _ in range(chunks)]
    influence = pl.pallas_call(
        functools.partial(kernel, sizes),
        out_shape=jax.ShapeDtypeStruct((blocks, LANES), F32),
        in_specs=[any_spec] * 4 + [vmem_spec] * 3 + [smem_spec] * 2,
        out_specs=vmem_spec,
        scratch_shapes=scratch,
        compiler_params=pltpu.CompilerParams(
            collective_id=0, has_side_effects=True, vmem_limit_bytes=61 * 1024 * 1024
        ),
    )(
        hidden_acts.T,
        out_grads,
        proj_in.T,
        proj_out.T,
        basis_in,
        basis_out,
        eigen_values,
        block_tokens,
        pair_list.T,
    )
    return influence.reshape(-1)


def solution(mesh):
    in_specs = (
        P(("grp", "doc"), ("proj", "sub")),
        P(("grp", "doc"), ("proj", "sub")),
        P(("proj", "sub"), None),
        P(("proj", "sub"), None),
        P(),
        P(),
        P(("proj", "sub"), None),
        P(("grp", "doc")),
        P(("grp", "doc"), None),
    )
    out_specs = P(("grp", "doc"))
    return jax.shard_map(body, mesh=mesh, in_specs=in_specs, out_specs=out_specs, check_vma=False)
```
